256 devices in a mesh: links: 64 (over x_hi, z, y), heads: 4 (over x_lo, core).
Axes of the slice: x: 4 (x_hi: 2, x_lo: 2; x = x_hi * 2 + x_lo), y: 4, z: 8, core: 2. Of those that a mesh axis runs over, the one named last changes fastest.
Arguments:
- queries: bfloat16 [65536, 512], P('links', 'heads'), may hold values from -6 to 6
- keys: bfloat16 [4096, 512], P('links', 'heads'), may hold values from -6 to 6
- values: bfloat16 [4096, 512], P('links', 'heads'), may hold values from -6 to 6
- attn: bfloat16 [65536, 512], P('links', 'heads'), may hold values from -6 to 6
- cotangent: bfloat16 [65536, 512], P('links', 'heads'), may hold values from -12 to 12
- out_weight: bfloat16 [512, 512], P('heads'), may hold values from -0.25 to 0.25
- lse: float32 [8, 65536], P('heads', 'links'), may hold values from 2 to 12
Outputs:
- query_grad: bfloat16 [65536, 512], P('links', 'heads')
- key_grad: bfloat16 [4096, 512], P('links', 'heads')
- value_grad: bfloat16 [4096, 512], P('links', 'heads')
The draws below stay inside these ranges and needn't reach their ends.
All inputs are finite; a program needn't handle non-finite values.
Results may differ from the reference program's by a relative error of at most 0.028.
Values may be sent and summed in bfloat16 or wider, within the bound.
A program may use at most 64 MiB of HBM per device.

```python
import math
import jax
import jax.numpy as jnp
from jax import lax

H = 8
DH = 64
D = 512
NQ = 65536
NZ = 4096


def draw_lse(key, part):
    key = jax.random.fold_in(key, 7)
    jitter = jax.random.uniform(key, (H, NQ), jnp.float32, -0.7, 0.7)
    return jnp.log(jnp.float32(NZ)) + 0.5 + jitter


def level_of(own_key, shape, cuts, smallest, top_value):
    def one(position, blocks):
        heights = jax.random.uniform(jax.random.fold_in(jax.random.fold_in(own_key, 6), position), (blocks,), jnp.float32, smallest / len(cuts), top_value / len(cuts))
        return jnp.repeat(jnp.exp(heights), shape[position] // blocks).reshape((-1,) + (1,) * (len(shape) - position - 1))

    level = one(*cuts[0])
    for cut in cuts[1:]:
        level = level * one(*cut)
    return level


def scatter_about(key, extent, scale, limit, cuts=(), held_as=jnp.bfloat16):
    loudness = level_of(key, extent, cuts, -0.22, 0.18) if cuts else 1.0
    array = jax.random.normal(key, extent, jnp.float32) * scale * loudness
    return jnp.minimum(jnp.maximum(array, -limit), limit).astype(held_as)


def setup_inputs(seed: int = 0) -> dict:
    streams_of = jax.random.split(jax.random.key(seed), 8)
    return {
        "queries": scatter_about(streams_of[0], (NQ, H * DH), 1.0, 6.0, ((0, 64), (1, 4))),
        "keys": scatter_about(streams_of[1], (NZ, H * DH), 1.0, 6.0, ((0, 64), (1, 4))),
        "values": scatter_about(streams_of[2], (NZ, H * DH), 1.0, 6.0, ((0, 64), (1, 4))),
        "attn": scatter_about(streams_of[3], (NQ, H * DH), 1.0, 6.0, ((0, 64), (1, 4))),
        "cotangent": scatter_about(streams_of[4], (NQ, D), 2.0, 12.0, ((0, 64), (1, 4))),
        "out_weight": scatter_about(streams_of[5], (H * DH, D), D ** -0.5, 0.25, ((0, 4),)),
        "lse": draw_lse(jax.random.fold_in(streams_of[7], 71), 0),
    }


def reference(queries, keys, values, attn, cotangent, out_weight, lse):
    count_q = queries.shape[0]
    count_k = keys.shape[0]
    d_attn = jnp.dot(cotangent, out_weight.T, preferred_element_type=jnp.float32).astype(jnp.bfloat16)
    query_all = queries.astype(jnp.float32).reshape(count_q, H, DH)
    grad_all = d_attn.astype(jnp.float32).reshape(count_q, H, DH)
    row_delta = jnp.sum(grad_all * attn.astype(jnp.float32).reshape(count_q, H, DH), -1).T
    key_all = keys.astype(jnp.float32).reshape(count_k, H, DH)
    value_all = values.astype(jnp.float32).reshape(count_k, H, DH)
    block = math.gcd(count_q, 1024)
    blocks = count_q // block

    def visit(carry, index):
        key_acc, value_acc = carry
        start = (index * block).astype(jnp.int32)
        query_rows = lax.dynamic_slice_in_dim(query_all, start, block, 0)
        grad_rows = lax.dynamic_slice_in_dim(grad_all, start, block, 0)
        saved = lax.dynamic_slice_in_dim(lse, start, block, 1)
        delta_rows = lax.dynamic_slice_in_dim(row_delta, start, block, 1)
        scores = jnp.einsum("qhd,khd->hqk", query_rows, key_all) * 0.125
        probs = jnp.exp(scores - saved[:, :, None])
        soft = lax.optimization_barrier(probs.astype(jnp.bfloat16)).astype(jnp.float32)
        dprob = jnp.einsum("qhd,khd->hqk", grad_rows, value_all)
        score_grads = (0.125 * probs * (dprob - delta_rows[:, :, None])).astype(jnp.bfloat16)
        score_grads = lax.optimization_barrier(score_grads).astype(jnp.float32)
        query_part = jnp.einsum("hqk,khd->qhd", score_grads, key_all).reshape(block, H * DH).astype(jnp.bfloat16)
        key_acc = key_acc + jnp.einsum("hqk,qhd->khd", score_grads, query_rows)
        value_acc = value_acc + jnp.einsum("hqk,qhd->khd", soft, grad_rows)
        return (key_acc, value_acc), query_part

    start_acc = (jnp.zeros((count_k, H, DH), jnp.float32), jnp.zeros((count_k, H, DH), jnp.float32))
    (key_acc, value_acc), query_parts = lax.scan(visit, start_acc, jnp.arange(blocks, dtype=jnp.int32))
    query_grad = query_parts.reshape(count_q, H * DH)
    key_grad = key_acc.reshape(count_k, H * DH).astype(jnp.bfloat16)
    value_grad = value_acc.reshape(count_k, H * DH).astype(jnp.bfloat16)
    return (query_grad, key_grad, value_grad)
```

```python
import jax
import jax.numpy as jnp
from jax import lax
from jax.experimental import pallas as pl
from jax.experimental.pallas import tpu as pltpu
from jax.sharding import PartitionSpec as P

F32, BF = jnp.float32, jnp.bfloat16
MESH = pl.DeviceIdType.MESH
LOG2E = 1.4426950408889634

XH, NZD, NYD = 2, 8, 4
ROWS = 1024
SHARD = 64
WIDTH = 128
DH = 64
CHUNK = 256
AUG = 256
ORDER = (4, 3, 5, 2, 6, 1, 7, 0)
PLACE = {r: i for i, r in enumerate(ORDER)}
YSTEP = (0, 1, 3, 2)
PIECES = 4
PROWS = ROWS // PIECES


def mm(a, b):
    return jnp.dot(a, b, preferred_element_type=F32)


def three(row):
    a = row.astype(BF).astype(F32)
    b = (row - a).astype(BF).astype(F32)
    return [a, b, row - a - b]


def aug_rows(row):
    return jnp.concatenate([*three(row), jnp.zeros((13, row.shape[1]), F32)], 0).astype(BF)


def kernel(
    q_in, k_in, v_in, attn_in, cot_in, w_in, lse_in,
    dq_out, dk_out, dv_out,
    cot, qa, da, lse2, delta2, qx, dx, kv, acc, psend, precv, zsend, zrecv, p_t, s_t, dq_t, dqs, dqr,
    cot_ss, cot_rs, z_ss, z_rs, y_ss, y_rs, x_ss, x_rs, r_ss, r_rs, g_ss, g_rs, dq_ss, dq_rs,
):
    link, head = lax.axis_index("links"), lax.axis_index("heads")
    xh, z, y = link // (NZD * NYD), (link // NYD) % NZD, link % NYD
    xl, core = head // 2, head % 2

    def at(dxh=0, dz=0, dy=0, dxl=0, dc=0):
        return (
            ((xh + dxh) % XH) * (NZD * NYD) + ((z + dz) % NZD) * NYD + (y + dy) % NYD,
            ((xl + dxl) % 2) * 2 + (core + dc) % 2,
        )

    def copy(src, dst, ss, rs, to):
        return pltpu.make_async_remote_copy(
            src_ref=src, dst_ref=dst, send_sem=ss, recv_sem=rs, device_id=to, device_id_type=MESH
        )

    def piece(i):
        return pl.ds(i * PROWS, PROWS)

    across = [
        copy(cot_in.at[piece(i)], cot.at[2, piece(i)], cot_ss.at[0, i], cot_rs.at[0, i], at(dxl=1))
        for i in range(PIECES)
    ]
    beside = copy(cot_in, cot.at[1], cot_ss.at[1, 0], cot_rs.at[1, 0], at(dc=1))
    onward = [
        copy(cot.at[2, piece(i)], cot.at[3, piece(i)], cot_ss.at[2, i], cot_rs.at[2, i], at(dc=1))
        for i in range(PIECES)
    ]
    shard = kv.at[0, PLACE[0]]
    along_z = {
        r: copy(shard, kv.at[0, PLACE[(NZD - r) % NZD]], z_ss.at[r], z_rs.at[r], at(dz=r))
        for r in (4, 3, 5, 2, 6, 1, 7)
    }
    along_y = {
        k: copy(kv.at[0], kv.at[k], y_ss.at[k], y_rs.at[k], at(dy=-YSTEP[k])) for k in (1, 2, 3)
    }
    swap_q = copy(q_in, qa.at[1], x_ss.at[0], x_rs.at[0], at(dxh=1))
    swap_l = copy(lse_in, lse2.at[1], x_ss.at[1], x_rs.at[1], at(dxh=1))
    swap_d = copy(delta2.at[0], delta2.at[1], x_ss.at[2], x_rs.at[2], at(dxh=1))
    swap_a = copy(da.at[0], da.at[1], x_ss.at[3], x_rs.at[3], at(dxh=1))
    back_y = {
        k: copy(psend.at[k - 1], precv.at[k - 1], r_ss.at[k], r_rs.at[k], at(dy=YSTEP[k]))
        for k in (1, 2, 3)
    }
    back_z = {
        r: copy(zsend.at[PLACE[r]], zrecv.at[r - 1], g_ss.at[r], g_rs.at[r], at(dz=r))
        for r in (4, 3, 5, 2, 6, 1, 7)
    }
    back_q = copy(dqs, dqr, dq_ss.at[0], dq_rs.at[0], at(dxh=1))

    for c in across:
        c.start()
    beside.start()
    kv[0, PLACE[0], 0] = k_in[...]
    kv[0, PLACE[0], 1] = v_in[...]
    for c in along_z.values():
        c.start()

    qa[0] = q_in[...]
    lse2[0] = lse_in[...]
    qx[...] = jnp.zeros_like(qx)
    dx[...] = jnp.zeros_like(dx)
    dq_t[...] = jnp.zeros_like(dq_t)
    acc[...] = jnp.zeros_like(acc)

    def widen_q(half):
        turned = qa[half].T
        for h in range(2):
            own = slice(DH * h, DH * h + DH)
            qx[half, h, own, :] = (turned[own].astype(F32) * 0.125).astype(BF)
            qx[half, h, WIDTH : WIDTH + 16, :] = aug_rows(lse2[half, h : h + 1, :])

    def widen_d(half, turned):
        for h in range(2):
            own = slice(DH * h, DH * h + DH)
            dx[half, h, own, :] = turned[own]
            dx[half, h, WIDTH : WIDTH + 16, :] = aug_rows(delta2[half, h : h + 1, :])

    widen_q(0)
    attn_t = attn_in[...].T

    for i in range(PIECES):
        across[i].wait_recv()
        onward[i].start()
    swap_q.start()
    swap_l.start()
    for c in along_z.values():
        c.wait_recv()
    for k in (1, 2, 3):
        along_y[k].start()
    beside.wait_recv()

    def block(dxl, dc):
        which = ((xl + dxl) % 2) * 2 + (core + dc) % 2
        return w_in[:, pl.ds(pl.multiple_of(which * WIDTH, WIDTH), WIDTH)]

    weight = jnp.concatenate([block(0, 0), block(0, 1), block(1, 0), block(1, 1)], 1)
    for i in range(PIECES):
        onward[i].wait_recv()
        rows = pl.ds(i * PROWS, PROWS)
        wide = jnp.concatenate([cot_in[rows, :], cot[1, rows], cot[2, rows], cot[3, rows]], 1)
        da[0, rows] = lax.dot_general(
            wide, weight, (((1,), (1,)), ((), ())), preferred_element_type=F32
        ).astype(BF)
    swap_a.start()
    turned = da[0].T
    product = turned.astype(F32) * attn_t.astype(F32)
    for h in range(2):
        delta2[0, h : h + 1, :] = jnp.sum(product[DH * h : DH * h + DH], axis=0, keepdims=True)
    swap_d.start()
    widen_d(0, turned)

    lane = lax.broadcasted_iota(jnp.int32, (CHUNK, WIDTH), 1)
    minus = jnp.where(lane < 3, -1.0, 0.0).astype(BF)
    left = lane < DH
    tile = 256

    def step(u, _):
        half, m = u // 8, u % 8
        k = half * 3 + (1 - 2 * half) * (m // 2)
        first = (m % 2) * 4

        for cls in (1, 2, 3):

            @pl.when(u == 2 * cls)
            def _():
                along_y[cls].wait_recv()

        @pl.when(u == 8)
        def _():
            swap_q.wait_recv()
            swap_l.wait_recv()
            swap_d.wait_recv()
            swap_a.wait_recv()
            widen_q(1)
            widen_d(1, da[1].T)

        places = pl.ds(first, 4)
        keys = kv[k, places, 0].reshape(CHUNK, WIDTH)
        values = kv[k, places, 1].reshape(CHUNK, WIDTH)
        wide_k = jnp.concatenate([keys, minus], 1)
        wide_v = jnp.concatenate([values, minus], 1)
        keys_t = keys.T
        outs = []
        for h in range(2):
            for j in range(ROWS // tile):
                cols = slice(j * tile, (j + 1) * tile)
                scores = mm(wide_k, qx[half, h, :, cols])
                moved = mm(wide_v, dx[half, h, :, cols])
                probs = jnp.exp2(scores * LOG2E)
                p_t[h, :, cols] = probs.astype(BF)
                s_t[h, :, cols] = (probs * moved).astype(BF)
            own = slice(DH * h, DH * h + DH)
            outs.append((mm(s_t[h], qa[half]), mm(p_t[h], da[half])))
            dq_t[half, own, :] += mm(keys_t[own], s_t[h])
        grad_k = jnp.where(left, outs[0][0], outs[1][0]) * 0.125
        grad_v = jnp.where(left, outs[0][1], outs[1][1])
        acc[k, places, 0] += grad_k.reshape(4, SHARD, WIDTH)
        acc[k, places, 1] += grad_v.reshape(4, SHARD, WIDTH)

        for cls in (3, 2, 1):

            @pl.when(u == 15 - 2 * cls)
            def _():
                psend[cls - 1] = acc[cls].astype(BF)
                back_y[cls].start()

        return 0

    lax.fori_loop(0, 16, step, 0)

    dqs[...] = (dq_t[1].T * 0.125).astype(BF)
    back_q.start()
    for cls in (3, 2, 1):
        back_y[cls].wait_recv()
    line = acc[0]
    for cls in (3, 2, 1):
        line = line + precv[cls - 1].astype(F32)
    acc[0] = line
    zsend[...] = line.astype(BF)
    for c in back_z.values():
        c.start()
    mine = (dq_t[0].T * 0.125).astype(F32)
    total = acc[0, PLACE[0]]
    for r, c in back_z.items():
        c.wait_recv()
        total = total + zrecv[r - 1].astype(F32)
    dk_out[...] = total[0].astype(BF)
    dv_out[...] = total[1].astype(BF)
    back_q.wait_recv()
    dq_out[...] = (mine + dqr[...].astype(F32)).astype(BF)

    for c in (
        *across, beside, *onward, *along_z.values(), *along_y.values(), swap_q, swap_l, swap_d, swap_a,
        *back_y.values(), *back_z.values(), back_q,
    ):
        c.wait_send()


def body(queries, keys, values, attn, cotangent, out_weight, lse):
    vmem = pl.BlockSpec(memory_space=pltpu.VMEM)
    dma = pltpu.SemaphoreType.DMA
    return pl.pallas_call(
        kernel,
        out_shape=[
            jax.ShapeDtypeStruct((ROWS, WIDTH), BF),
            jax.ShapeDtypeStruct((SHARD, WIDTH), BF),
            jax.ShapeDtypeStruct((SHARD, WIDTH), BF),
        ],
        in_specs=[vmem] * 7,
        out_specs=[vmem] * 3,
        scratch_shapes=[
            pltpu.VMEM((4, ROWS, WIDTH), BF),
            pltpu.VMEM((2, ROWS, WIDTH), BF),
            pltpu.VMEM((2, ROWS, WIDTH), BF),
            pltpu.VMEM((2, 2, ROWS), F32),
            pltpu.VMEM((2, 2, ROWS), F32),
            pltpu.VMEM((2, 2, AUG, ROWS), BF),
            pltpu.VMEM((2, 2, AUG, ROWS), BF),
            pltpu.VMEM((4, NZD, 2, SHARD, WIDTH), BF),
            pltpu.VMEM((4, NZD, 2, SHARD, WIDTH), F32),
            pltpu.VMEM((3, NZD, 2, SHARD, WIDTH), BF),
            pltpu.VMEM((3, NZD, 2, SHARD, WIDTH), BF),
            pltpu.VMEM((NZD, 2, SHARD, WIDTH), BF),
            pltpu.VMEM((NZD - 1, 2, SHARD, WIDTH), BF),
            pltpu.VMEM((2, CHUNK, ROWS), BF),
            pltpu.VMEM((2, CHUNK, ROWS), BF),
            pltpu.VMEM((2, WIDTH, ROWS), F32),
            pltpu.VMEM((ROWS, WIDTH), BF),
            pltpu.VMEM((ROWS, WIDTH), BF),
            dma((3, PIECES)), dma((3, PIECES)),
            dma((NZD,)), dma((NZD,)),
            dma((4,)), dma((4,)),
            dma((4,)), dma((4,)),
            dma((4,)), dma((4,)),
            dma((NZD,)), dma((NZD,)),
            dma((1,)), dma((1,)),
        ],
        compiler_params=pltpu.CompilerParams(
            has_side_effects=True, vmem_limit_bytes=48 * 2**20
        ),
        cost_estimate=pl.CostEstimate(
            flops=11 * 10**9, bytes_accessed=3 * 2**20, transcendentals=2**23
        ),
    )(queries, keys, values, attn, cotangent, out_weight, lse)


def solution(mesh):
    in_specs = (
        P("links", "heads"),
        P("links", "heads"),
        P("links", "heads"),
        P("links", "heads"),
        P("links", "heads"),
        P("heads", None),
        P("heads", "links"),
    )
    out_specs = (P("links", "heads"), P("links", "heads"), P("links", "heads"))
    return jax.shard_map(body, mesh=mesh, in_specs=in_specs, out_specs=out_specs, check_vma=False)
```

```python
import jax
import jax.numpy as jnp
from jax import lax
from jax.experimental import pallas as pl
from jax.experimental.pallas import tpu as pltpu
from jax.sharding import PartitionSpec as P

F32, BF = jnp.float32, jnp.bfloat16
MESH = pl.DeviceIdType.MESH
LOG2E = 1.4426950408889634

XH, NZD, NYD = 2, 8, 4
ROWS = 1024
SHARD = 64
WIDTH = 128
DH = 64
CHUNK = 256
AUG = 256
ORDER = (4, 3, 5, 2, 6, 1, 7, 0)
PLACE = {r: i for i, r in enumerate(ORDER)}
YSTEP = (0, 1, 3, 2)
FAR, NEAR = 0, 1
UNITS = (
    (0, 0, FAR), (0, 1, NEAR), (0, 2, NEAR), (0, 1, FAR), (0, 2, FAR), (0, 3, NEAR), (0, 3, FAR),
    (1, 3, FAR), (1, 1, FAR), (1, 2, FAR), (1, 0, FAR), (1, 3, NEAR), (1, 1, NEAR), (1, 2, NEAR), (1, 0, NEAR),
    (0, 0, NEAR),
)
TURN = {unit: i for i, unit in enumerate(UNITS)}
HALF_R = {FAR: (4, 3, 5, 2), NEAR: (6, 1, 7)}
PIECES = 4
PROWS = ROWS // PIECES


def mm(a, b):
    return jnp.dot(a, b, preferred_element_type=F32)


def three(row):
    a = row.astype(BF).astype(F32)
    b = (row - a).astype(BF).astype(F32)
    return [a, b, row - a - b]


def aug_rows(row):
    return jnp.concatenate([*three(row), jnp.zeros((13, row.shape[1]), F32)], 0).astype(BF)


def kernel(
    q_in, k_in, v_in, attn_in, cot_in, w_in, lse_in,
    dq_out, dk_out, dv_out,
    attn, w, in_sem, cot, qa, da, lse2, delta2, qx, dx, kv, acc, psend, precv, zsend, zrecv, p_t, s_t, dq_t, dqs, dqr,
    cot_ss, cot_rs, z_ss, z_rs, y_ss, y_rs, x_ss, x_rs, r_ss, r_rs, g_ss, g_rs, dq_ss, dq_rs,
):
    link, head = lax.axis_index("links"), lax.axis_index("heads")
    xh, z, y = link // (NZD * NYD), (link // NYD) % NZD, link % NYD
    xl, core = head // 2, head % 2

    def at(dxh=0, dz=0, dy=0, dxl=0, dc=0):
        return (
            ((xh + dxh) % XH) * (NZD * NYD) + ((z + dz) % NZD) * NYD + (y + dy) % NYD,
            ((xl + dxl) % 2) * 2 + (core + dc) % 2,
        )

    def copy(src, dst, ss, rs, to):
        return pltpu.make_async_remote_copy(
            src_ref=src, dst_ref=dst, send_sem=ss, recv_sem=rs, device_id=to, device_id_type=MESH
        )

    def piece(i):
        return pl.ds(i * PROWS, PROWS)

    def half_at(p):
        return pl.ds(p * 4, 4)

    partners = [at(dz=r) for r in range(1, NZD)] + [at(dy=r) for r in range(1, NYD)]
    partners += [at(dxh=1), at(dxl=1), at(dc=1)]
    barrier = pltpu.get_barrier_semaphore()
    for to in partners:
        pl.semaphore_signal(barrier, inc=1, device_id=to, device_id_type=MESH)
    places = (
        (k_in, kv.at[0, PLACE[0], 0]), (v_in, kv.at[0, PLACE[0], 1]), (q_in, qa.at[0]),
        (attn_in, attn), (lse_in, lse2.at[0]), (w_in, w), (cot_in, cot.at[0]),
    )
    fetch = [pltpu.make_async_copy(src, dst, in_sem.at[i]) for i, (src, dst) in enumerate(places)]
    for c in fetch:
        c.start()

    across = [
        copy(cot_in.at[piece(i)], cot.at[2, piece(i)], cot_ss.at[0, i], cot_rs.at[0, i], at(dxl=1))
        for i in range(PIECES)
    ]
    beside = copy(cot_in, cot.at[1], cot_ss.at[1, 0], cot_rs.at[1, 0], at(dc=1))
    onward = [
        copy(cot.at[2, piece(i)], cot.at[3, piece(i)], cot_ss.at[2, i], cot_rs.at[2, i], at(dc=1))
        for i in range(PIECES)
    ]
    shard = kv.at[0, PLACE[0]]
    along_z = {
        r: copy(shard, kv.at[0, PLACE[(NZD - r) % NZD]], z_ss.at[r], z_rs.at[r], at(dz=r))
        for r in (4, 3, 5, 2, 6, 1, 7)
    }
    along_y = {
        (k, p): copy(kv.at[0, half_at(p)], kv.at[k, half_at(p)], y_ss.at[k, p], y_rs.at[k, p], at(dy=-YSTEP[k]))
        for k in (1, 2, 3) for p in (NEAR, FAR)
    }
    swap_q = copy(q_in, qa.at[1], x_ss.at[0], x_rs.at[0], at(dxh=1))
    swap_l = copy(lse_in, lse2.at[1], x_ss.at[1], x_rs.at[1], at(dxh=1))
    swap_d = copy(delta2.at[0], delta2.at[1], x_ss.at[2], x_rs.at[2], at(dxh=1))
    swap_a = copy(da.at[0], da.at[1], x_ss.at[3], x_rs.at[3], at(dxh=1))
    back_y = {
        (k, p): copy(
            psend.at[k - 1, half_at(p)], precv.at[k - 1, half_at(p)], r_ss.at[k, p], r_rs.at[k, p], at(dy=YSTEP[k])
        )
        for k in (1, 2, 3) for p in (FAR, NEAR)
    }
    back_z = {
        r: copy(zsend.at[PLACE[r]], zrecv.at[r - 1], g_ss.at[r], g_rs.at[r], at(dz=r))
        for r in (4, 3, 5, 2, 6, 1, 7)
    }
    back_q = copy(dqs, dqr, dq_ss.at[0], dq_rs.at[0], at(dxh=1))

    pl.semaphore_wait(barrier, len(partners))
    for c in across:
        c.start()
    fetch[0].wait()
    fetch[1].wait()
    for p in (NEAR, FAR):
        for r in HALF_R[p]:
            along_z[NZD - r].start()
    beside.start()
    fetch[2].wait()
    fetch[4].wait()
    qx[...] = jnp.zeros_like(qx)
    dx[...] = jnp.zeros_like(dx)
    dq_t[...] = jnp.zeros_like(dq_t)
    acc[...] = jnp.zeros_like(acc)

    def widen_q(half):
        turned = qa[half].T
        for h in range(2):
            own = slice(DH * h, DH * h + DH)
            qx[half, h, own, :] = (turned[own].astype(F32) * 0.125).astype(BF)
            qx[half, h, WIDTH : WIDTH + 16, :] = aug_rows(lse2[half, h : h + 1, :])

    def widen_d(half, turned):
        for h in range(2):
            own = slice(DH * h, DH * h + DH)
            dx[half, h, own, :] = turned[own]
            dx[half, h, WIDTH : WIDTH + 16, :] = aug_rows(delta2[half, h : h + 1, :])

    widen_q(0)
    fetch[3].wait()
    attn_t = attn[...].T

    def pass_on(i):
        across[i].wait_recv()
        onward[i].start()

    def spread(p):
        for r in HALF_R[p]:
            along_z[NZD - r].wait_recv()
        for k in (1, 2):
            along_y[k, p].start()

    pass_on(0)
    spread(NEAR)
    pass_on(1)
    pass_on(2)
    pass_on(3)
    spread(FAR)
    swap_q.start()
    swap_l.start()
    fetch[5].wait()
    fetch[6].wait()
    beside.wait_recv()

    def block(dxl, dc):
        which = ((xl + dxl) % 2) * 2 + (core + dc) % 2
        return w[:, pl.ds(pl.multiple_of(which * WIDTH, WIDTH), WIDTH)]

    weight = jnp.concatenate([block(0, 0), block(0, 1), block(1, 0), block(1, 1)], 1)
    for i in range(PIECES):
        onward[i].wait_recv()
        rows = pl.ds(i * PROWS, PROWS)
        wide = jnp.concatenate([cot[0, rows], cot[1, rows], cot[2, rows], cot[3, rows]], 1)
        da[0, rows] = lax.dot_general(
            wide, weight, (((1,), (1,)), ((), ())), preferred_element_type=F32
        ).astype(BF)
    swap_a.start()
    turned = da[0].T
    product = turned.astype(F32) * attn_t.astype(F32)
    for h in range(2):
        delta2[0, h : h + 1, :] = jnp.sum(product[DH * h : DH * h + DH], axis=0, keepdims=True)
    swap_d.start()
    widen_d(0, turned)

    lane = lax.broadcasted_iota(jnp.int32, (CHUNK, WIDTH), 1)
    minus = jnp.where(lane < 3, -1.0, 0.0).astype(BF)
    left = lane < DH
    tile = 256

    def step(u, _):
        def pick(column):
            return sum(jnp.where(u == i, unit[column], 0) for i, unit in enumerate(UNITS) if unit[column])

        half, k, first = pick(0), pick(1), pick(2) * 4

        @pl.when(u == 1)
        def _():
            along_y[3, NEAR].start()
            along_y[3, FAR].start()

        for cls, p in along_y:

            @pl.when(u == TURN[0, cls, p])
            def _():
                along_y[cls, p].wait_recv()

        @pl.when(u == UNITS.index((1, 3, FAR)))
        def _():
            swap_q.wait_recv()
            swap_l.wait_recv()
            swap_d.wait_recv()
            swap_a.wait_recv()
            widen_q(1)
            widen_d(1, da[1].T)

        places = pl.ds(first, 4)
        keys = kv[k, places, 0].reshape(CHUNK, WIDTH)
        values = kv[k, places, 1].reshape(CHUNK, WIDTH)
        wide_k = jnp.concatenate([keys, minus], 1)
        wide_v = jnp.concatenate([values, minus], 1)
        keys_t = keys.T
        outs = []
        for h in range(2):
            for j in range(ROWS // tile):
                cols = slice(j * tile, (j + 1) * tile)
                scores = mm(wide_k, qx[half, h, :, cols])
                moved = mm(wide_v, dx[half, h, :, cols])
                probs = jnp.exp2(scores * LOG2E)
                p_t[h, :, cols] = probs.astype(BF)
                s_t[h, :, cols] = (probs * moved).astype(BF)
            own = slice(DH * h, DH * h + DH)
            outs.append((mm(s_t[h], qa[half]), mm(p_t[h], da[half])))
            dq_t[half, own, :] += mm(keys_t[own], s_t[h])
        grad_k = jnp.where(left, outs[0][0], outs[1][0]) * 0.125
        grad_v = jnp.where(left, outs[0][1], outs[1][1])
        acc[k, places, 0] += grad_k.reshape(4, SHARD, WIDTH)
        acc[k, places, 1] += grad_v.reshape(4, SHARD, WIDTH)

        for cls, p in back_y:

            @pl.when(u == TURN[1, cls, p])
            def _():
                psend[cls - 1, half_at(p)] = acc[cls, half_at(p)].astype(BF)
                back_y[cls, p].start()

        @pl.when(u == TURN[1, 0, NEAR])
        def _():
            dqs[...] = (dq_t[1].T * 0.125).astype(BF)
            back_q.start()
            gather(FAR)

        return 0

    def gather(p):
        half = half_at(p)
        for cls in (3, 1, 2):
            back_y[cls, p].wait_recv()
        line = acc[0, half]
        for cls in (3, 1, 2):
            line = line + precv[cls - 1, half].astype(F32)
        acc[0, half] = line
        zsend[half] = line.astype(BF)
        for r in HALF_R[p]:
            back_z[r].start()

    lax.fori_loop(0, len(UNITS), step, 0)

    gather(NEAR)
    mine = dq_t[0].T * 0.125
    total = acc[0, PLACE[0]]
    for r in HALF_R[FAR] + HALF_R[NEAR]:
        back_z[r].wait_recv()
        total = total + zrecv[r - 1].astype(F32)
    dk_out[...] = total[0].astype(BF)
    dv_out[...] = total[1].astype(BF)
    back_q.wait_recv()
    dq_out[...] = (mine + dqr[...].astype(F32)).astype(BF)

    for c in (
        *across, beside, *onward, *along_z.values(), *along_y.values(), swap_q, swap_l, swap_d, swap_a,
        *back_y.values(), *back_z.values(), back_q,
    ):
        c.wait_send()


def body(queries, keys, values, attn, cotangent, out_weight, lse):
    vmem = pl.BlockSpec(memory_space=pltpu.VMEM)
    dma = pltpu.SemaphoreType.DMA
    return pl.pallas_call(
        kernel,
        out_shape=[
            jax.ShapeDtypeStruct((ROWS, WIDTH), BF),
            jax.ShapeDtypeStruct((SHARD, WIDTH), BF),
            jax.ShapeDtypeStruct((SHARD, WIDTH), BF),
        ],
        in_specs=[pl.BlockSpec(memory_space=pl.ANY)] * 7,
        out_specs=[vmem] * 3,
        scratch_shapes=[
            pltpu.VMEM((ROWS, WIDTH), BF),
            pltpu.VMEM((WIDTH, 4 * WIDTH), BF),
            dma((7,)),
            pltpu.VMEM((4, ROWS, WIDTH), BF),
            pltpu.VMEM((2, ROWS, WIDTH), BF),
            pltpu.VMEM((2, ROWS, WIDTH), BF),
            pltpu.VMEM((2, 2, ROWS), F32),
            pltpu.VMEM((2, 2, ROWS), F32),
            pltpu.VMEM((2, 2, AUG, ROWS), BF),
            pltpu.VMEM((2, 2, AUG, ROWS), BF),
            pltpu.VMEM((4, NZD, 2, SHARD, WIDTH), BF),
            pltpu.VMEM((4, NZD, 2, SHARD, WIDTH), F32),
            pltpu.VMEM((3, NZD, 2, SHARD, WIDTH), BF),
            pltpu.VMEM((3, NZD, 2, SHARD, WIDTH), BF),
            pltpu.VMEM((NZD, 2, SHARD, WIDTH), BF),
            pltpu.VMEM((NZD - 1, 2, SHARD, WIDTH), BF),
            pltpu.VMEM((2, CHUNK, ROWS), BF),
            pltpu.VMEM((2, CHUNK, ROWS), BF),
            pltpu.VMEM((2, WIDTH, ROWS), F32),
            pltpu.VMEM((ROWS, WIDTH), BF),
            pltpu.VMEM((ROWS, WIDTH), BF),
            dma((3, PIECES)), dma((3, PIECES)),
            dma((NZD,)), dma((NZD,)),
            dma((4, 2)), dma((4, 2)),
            dma((4,)), dma((4,)),
            dma((4, 2)), dma((4, 2)),
            dma((NZD,)), dma((NZD,)),
            dma((1,)), dma((1,)),
        ],
        compiler_params=pltpu.CompilerParams(
            collective_id=0, has_side_effects=True, vmem_limit_bytes=56 * 2**20
        ),
        cost_estimate=pl.CostEstimate(
            flops=11 * 10**9, bytes_accessed=3 * 2**20, transcendentals=2**23
        ),
    )(queries, keys, values, attn, cotangent, out_weight, lse)


def solution(mesh):
    in_specs = (
        P("links", "heads"),
        P("links", "heads"),
        P("links", "heads"),
        P("links", "heads"),
        P("links", "heads"),
        P("heads", None),
        P("heads", "links"),
    )
    out_specs = (P("links", "heads"), P("links", "heads"), P("links", "heads"))
    return jax.shard_map(body, mesh=mesh, in_specs=in_specs, out_specs=out_specs, check_vma=False)
```

```python
import jax
import jax.numpy as jnp
from jax import lax
from jax.experimental import pallas as pl
from jax.experimental.pallas import tpu as pltpu
from jax.sharding import PartitionSpec as P

F32, BF = jnp.float32, jnp.bfloat16
MESH = pl.DeviceIdType.MESH
LOG2E = 1.4426950408889634

XH, NZD, NYD = 2, 8, 4
ROWS = 1024
SHARD = 64
WIDTH = 128
DH = 64
CHUNK = 256
AUG = 256
ORDER = (4, 3, 5, 2, 6, 1, 7, 0)
PLACE = {r: i for i, r in enumerate(ORDER)}
YSTEP = (0, 1, 3, 2)
FAR, NEAR = 0, 1
UNITS = (
    (0, 0, FAR), (0, 1, NEAR), (0, 2, NEAR), (0, 1, FAR), (0, 2, FAR), (0, 3, NEAR), (0, 3, FAR),
    (1, 3, FAR), (1, 1, FAR), (1, 2, FAR), (1, 0, FAR), (1, 3, NEAR), (1, 1, NEAR), (1, 2, NEAR), (1, 0, NEAR),
    (0, 0, NEAR),
)
TILE = 256
FIRST_SWAPPED = [half for half, _, _ in UNITS].index(1)
TURN = {unit: i for i, unit in enumerate(UNITS)}
HALF_R = {FAR: (4, 3, 5, 2), NEAR: (6, 1, 7)}
PIECES = 4
PROWS = ROWS // PIECES


def mm(a, b):
    return jnp.dot(a, b, preferred_element_type=F32)


def nt(a, b):
    return lax.dot_general(a, b, (((1,), (1,)), ((), ())), preferred_element_type=F32)


def three(row):
    a = row.astype(BF).astype(F32)
    b = (row - a).astype(BF).astype(F32)
    return [a, b, row - a - b]


def columns(rows):
    n = rows.shape[1]
    pad = jnp.zeros((5, n), F32)
    parts = [p for h in range(2) for p in (*three(rows[h : h + 1, :]), pad)]
    low = jnp.concatenate(parts, 0).astype(BF)
    return jnp.concatenate([low, jnp.zeros((WIDTH - 16, n), BF)], 0).T


def kernel(
    q_in, k_in, v_in, attn_in, cot_in, w_in, lse_in,
    dq_out, dk_out, dv_out,
    attn, w, in_sem, cot, qa, da, lse2, delta2, qx, dx, q_t, d_t, kv, acc, psend, precv, zsend, zrecv, owned,
    probs, grads, dq, dqs, dqr,
    cot_ss, cot_rs, z_ss, z_rs, y_ss, y_rs, x_ss, x_rs, r_ss, r_rs, g_ss, g_rs, dq_ss, dq_rs,
):
    link, head = lax.axis_index("links"), lax.axis_index("heads")
    xh, z, y = link // (NZD * NYD), (link // NYD) % NZD, link % NYD
    xl, core = head // 2, head % 2

    def at(dxh=0, dz=0, dy=0, dxl=0, dc=0):
        return (
            ((xh + dxh) % XH) * (NZD * NYD) + ((z + dz) % NZD) * NYD + (y + dy) % NYD,
            ((xl + dxl) % 2) * 2 + (core + dc) % 2,
        )

    def copy(src, dst, ss, rs, to):
        return pltpu.make_async_remote_copy(
            src_ref=src, dst_ref=dst, send_sem=ss, recv_sem=rs, device_id=to, device_id_type=MESH
        )

    def piece(i):
        return pl.ds(i * PROWS, PROWS)

    def half_at(p):
        return pl.ds(p * 4, 4)

    partners = [at(dz=r) for r in range(1, NZD)] + [at(dy=r) for r in range(1, NYD)]
    partners += [at(dxh=1), at(dxl=1), at(dc=1)]
    barrier = pltpu.get_barrier_semaphore()
    for to in partners:
        pl.semaphore_signal(barrier, inc=1, device_id=to, device_id_type=MESH)
    places = (
        (k_in, kv.at[0, PLACE[0], 0]), (v_in, kv.at[0, PLACE[0], 1]), (q_in, qa.at[0]),
        (attn_in, attn), (lse_in, lse2.at[0]), (w_in, w), (cot_in, cot.at[0]),
    )
    fetch = [pltpu.make_async_copy(src, dst, in_sem.at[i]) for i, (src, dst) in enumerate(places)]
    for c in fetch:
        c.start()

    across = [
        copy(cot_in.at[piece(i)], cot.at[2, piece(i)], cot_ss.at[0, i], cot_rs.at[0, i], at(dxl=1))
        for i in range(PIECES)
    ]
    beside = copy(cot_in, cot.at[1], cot_ss.at[1, 0], cot_rs.at[1, 0], at(dc=1))
    onward = [
        copy(cot.at[2, piece(i)], cot.at[3, piece(i)], cot_ss.at[2, i], cot_rs.at[2, i], at(dc=1))
        for i in range(PIECES)
    ]
    shard = kv.at[0, PLACE[0]]
    along_z = {
        r: copy(shard, kv.at[0, PLACE[(NZD - r) % NZD]], z_ss.at[r], z_rs.at[r], at(dz=r))
        for r in (4, 3, 5, 2, 6, 1, 7)
    }
    along_y = {
        (k, p): copy(kv.at[0, half_at(p)], kv.at[k, half_at(p)], y_ss.at[k, p], y_rs.at[k, p], at(dy=-YSTEP[k]))
        for k in (1, 2, 3) for p in (NEAR, FAR)
    }
    swap_q = copy(q_in, qa.at[1], x_ss.at[0], x_rs.at[0], at(dxh=1))
    swap_l = copy(lse_in, lse2.at[1], x_ss.at[1], x_rs.at[1], at(dxh=1))
    swap_d = copy(delta2.at[0], delta2.at[1], x_ss.at[2], x_rs.at[2], at(dxh=1))
    swap_a = copy(da.at[0], da.at[1], x_ss.at[3], x_rs.at[3], at(dxh=1))
    back_y = {
        (k, p): copy(
            psend.at[k - 1, p], precv.at[k - 1, p], r_ss.at[k, p], r_rs.at[k, p], at(dy=YSTEP[k])
        )
        for k in (1, 2, 3) for p in (FAR, NEAR)
    }
    back_z = {
        r: copy(zsend.at[PLACE[r]], zrecv.at[r - 1], g_ss.at[r], g_rs.at[r], at(dz=r))
        for r in (4, 3, 5, 2, 6, 1, 7)
    }
    back_q = copy(dqs, dqr, dq_ss.at[0], dq_rs.at[0], at(dxh=1))

    pl.semaphore_wait(barrier, len(partners))
    for c in across:
        c.start()
    fetch[0].wait()
    fetch[1].wait()
    for p in (NEAR, FAR):
        for r in HALF_R[p]:
            along_z[NZD - r].start()
    beside.start()
    fetch[2].wait()
    fetch[4].wait()
    dq[...] = jnp.zeros_like(dq)
    acc[...] = jnp.zeros_like(acc)

    lane = lax.broadcasted_iota(jnp.int32, (1, WIDTH), 1)

    def one_head(h):
        return jnp.where(lane // DH == h, 1.0, 0.0)

    def one_group(h):
        return jnp.where(lane // 8 == h, 1.0, 0.0).astype(BF)

    def widen_q(half):
        tokens = qa[half]
        q_t[half] = (tokens * jnp.full((1, WIDTH), 0.125, BF)).T
        extra = columns(lse2[half])
        for h in range(2):
            qx[half, h, :, :WIDTH] = tokens * (one_head(h) * 0.125).astype(BF)
            qx[half, h, :, WIDTH:] = extra * one_group(h)

    def widen_d(half, rows, tokens):
        extra = columns(delta2[half, :, rows])
        for h in range(2):
            dx[half, h, rows, :WIDTH] = tokens * one_head(h).astype(BF)
            dx[half, h, rows, WIDTH:] = extra * one_group(h)

    widen_q(0)
    fetch[3].wait()
    attn_t = attn[...].T

    def pass_on(i):
        across[i].wait_recv()
        onward[i].start()

    def spread(p):
        for r in HALF_R[p]:
            along_z[NZD - r].wait_recv()
        for k in (1, 2):
            along_y[k, p].start()

    pass_on(0)
    spread(NEAR)
    pass_on(1)
    pass_on(2)
    pass_on(3)
    spread(FAR)
    swap_q.start()
    swap_l.start()
    fetch[5].wait()
    fetch[6].wait()
    beside.wait_recv()

    def block(dxl, dc):
        which = ((xl + dxl) % 2) * 2 + (core + dc) % 2
        return w[:, pl.ds(pl.multiple_of(which * WIDTH, WIDTH), WIDTH)]

    weight = jnp.concatenate([block(0, 0), block(0, 1), block(1, 0), block(1, 1)], 1)
    row = lax.broadcasted_iota(jnp.int32, (WIDTH, CHUNK), 0)
    minus = jnp.where(row < 16, -1.0, 0.0).astype(BF)
    left = lax.broadcasted_iota(jnp.int32, (TILE, WIDTH), 1) < DH
    tiles = range(ROWS // TILE)

    def unit(half, k, p):
        places = pl.ds(p * 4, 4)
        keys = kv[k, places, 0].reshape(CHUNK, WIDTH)
        values = kv[k, places, 1].reshape(CHUNK, WIDTH)
        right_k = jnp.concatenate([keys.T, minus], 0)
        right_v = jnp.concatenate([values.T, minus], 0)

        def tile(h, j):
            rows = slice(j * TILE, (j + 1) * TILE)
            scores = mm(qx[half, h, rows, :], right_k)
            moved = mm(dx[half, h, rows, :], right_v)
            prob = jnp.exp2(scores * LOG2E)
            probs[h, rows, :] = prob.astype(BF)
            grads[h, rows, :] = (prob * moved).astype(BF)

        def zones(h):
            own = slice(DH * h, DH * h + DH)
            acc[k, p, 0, own, :] += mm(q_t[half, own, :], grads[h])
            acc[k, p, 1, own, :] += mm(d_t[half, own, :], probs[h])

        def links(j):
            rows = slice(j * TILE, (j + 1) * TILE)
            dq[half, rows, :] += jnp.where(left, mm(grads[0, rows, :], keys), mm(grads[1, rows, :], keys))

        return tile, zones, links

    tile, zones, links = unit(*UNITS[0])
    for i in range(PIECES):
        onward[i].wait_recv()
        rows = pl.ds(i * PROWS, PROWS)
        wide = jnp.concatenate([cot[0, rows], cot[1, rows], cot[2, rows], cot[3, rows]], 1)
        tokens = nt(wide, weight).astype(BF)
        da[0, rows] = tokens
        turned = tokens.T
        d_t[0, :, rows] = turned
        product = turned.astype(F32) * attn_t[:, i * PROWS : (i + 1) * PROWS].astype(F32)
        for h in range(2):
            delta2[0, h : h + 1, rows] = jnp.sum(product[DH * h : DH * h + DH], axis=0, keepdims=True)
        widen_d(0, rows, tokens)
        for h in range(2):
            tile(h, i)
    swap_a.start()
    swap_d.start()
    for h in range(2):
        zones(h)
    for j in tiles:
        links(j)

    def step(u, _):
        def pick(column):
            return sum(jnp.where(u == i, unit[column], 0) for i, unit in enumerate(UNITS) if unit[column])

        half, k, p = pick(0), pick(1), pick(2)

        @pl.when(u == 1)
        def _():
            along_y[3, NEAR].start()
            along_y[3, FAR].start()

        for cls, part in along_y:

            @pl.when(u == TURN[0, cls, part])
            def _():
                along_y[cls, part].wait_recv()

        @pl.when(u == FIRST_SWAPPED)
        def _():
            swap_q.wait_recv()
            swap_l.wait_recv()
            swap_d.wait_recv()
            swap_a.wait_recv()
            widen_q(1)
            tokens = da[1]
            d_t[1] = tokens.T
            widen_d(1, pl.ds(0, ROWS), tokens)

        tile, zones, links = unit(half, k, p)
        for j in tiles:
            tile(0, j)
        tile(1, 0)
        zones(0)
        for j in tiles[1:]:
            tile(1, j)
        zones(1)
        for j in tiles:
            links(j)

        for cls, p in back_y:

            @pl.when(u == TURN[1, cls, p])
            def _():
                psend[cls - 1, p] = acc[cls, p].astype(BF)
                back_y[cls, p].start()

        @pl.when(u == TURN[1, 0, NEAR])
        def _():
            dqs[...] = (dq[1] * 0.125).astype(BF)
            back_q.start()
            gather(FAR)

        return 0

    def gather(p):
        for cls in (3, 1, 2):
            back_y[cls, p].wait_recv()
        for t in range(2):
            line = acc[0, p, t]
            for cls in (3, 1, 2):
                line = line + precv[cls - 1, p, t].astype(F32)
            shards = line.T.reshape(4, SHARD, WIDTH)
            zsend[half_at(p), t] = shards.astype(BF)
            if p == NEAR:
                owned[t] = shards[PLACE[0] - 4]
        for r in HALF_R[p]:
            back_z[r].start()

    lax.fori_loop(1, len(UNITS), step, 0)

    gather(NEAR)
    total = owned[...]
    for r in HALF_R[FAR] + HALF_R[NEAR]:
        back_z[r].wait_recv()
        total = total + zrecv[r - 1].astype(F32)
    dk_out[...] = total[0].astype(BF)
    dv_out[...] = total[1].astype(BF)
    back_q.wait_recv()
    dq_out[...] = (dq[0] * 0.125 + dqr[...].astype(F32)).astype(BF)

    for c in (
        *across, beside, *onward, *along_z.values(), *along_y.values(), swap_q, swap_l, swap_d, swap_a,
        *back_y.values(), *back_z.values(), back_q,
    ):
        c.wait_send()


def body(queries, keys, values, attn, cotangent, out_weight, lse):
    vmem = pl.BlockSpec(memory_space=pltpu.VMEM)
    dma = pltpu.SemaphoreType.DMA
    return pl.pallas_call(
        kernel,
        out_shape=[
            jax.ShapeDtypeStruct((ROWS, WIDTH), BF),
            jax.ShapeDtypeStruct((SHARD, WIDTH), BF),
            jax.ShapeDtypeStruct((SHARD, WIDTH), BF),
        ],
        in_specs=[pl.BlockSpec(memory_space=pl.ANY)] * 7,
        out_specs=[vmem] * 3,
        scratch_shapes=[
            pltpu.VMEM((ROWS, WIDTH), BF),
            pltpu.VMEM((WIDTH, 4 * WIDTH), BF),
            dma((7,)),
            pltpu.VMEM((4, ROWS, WIDTH), BF),
            pltpu.VMEM((2, ROWS, WIDTH), BF),
            pltpu.VMEM((2, ROWS, WIDTH), BF),
            pltpu.VMEM((2, 2, ROWS), F32),
            pltpu.VMEM((2, 2, ROWS), F32),
            pltpu.VMEM((2, 2, ROWS, AUG), BF),
            pltpu.VMEM((2, 2, ROWS, AUG), BF),
            pltpu.VMEM((2, WIDTH, ROWS), BF),
            pltpu.VMEM((2, WIDTH, ROWS), BF),
            pltpu.VMEM((4, NZD, 2, SHARD, WIDTH), BF),
            pltpu.VMEM((4, 2, 2, WIDTH, CHUNK), F32),
            pltpu.VMEM((3, 2, 2, WIDTH, CHUNK), BF),
            pltpu.VMEM((3, 2, 2, WIDTH, CHUNK), BF),
            pltpu.VMEM((NZD, 2, SHARD, WIDTH), BF),
            pltpu.VMEM((NZD - 1, 2, SHARD, WIDTH), BF),
            pltpu.VMEM((2, SHARD, WIDTH), F32),
            pltpu.VMEM((2, ROWS, CHUNK), BF),
            pltpu.VMEM((2, ROWS, CHUNK), BF),
            pltpu.VMEM((2, ROWS, WIDTH), F32),
            pltpu.VMEM((ROWS, WIDTH), BF),
            pltpu.VMEM((ROWS, WIDTH), BF),
            dma((3, PIECES)), dma((3, PIECES)),
            dma((NZD,)), dma((NZD,)),
            dma((4, 2)), dma((4, 2)),
            dma((4,)), dma((4,)),
            dma((4, 2)), dma((4, 2)),
            dma((NZD,)), dma((NZD,)),
            dma((1,)), dma((1,)),
        ],
        compiler_params=pltpu.CompilerParams(
            collective_id=0, has_side_effects=True, vmem_limit_bytes=56 * 2**20
        ),
        cost_estimate=pl.CostEstimate(
            flops=11 * 10**9, bytes_accessed=3 * 2**20, transcendentals=2**23
        ),
    )(queries, keys, values, attn, cotangent, out_weight, lse)


def solution(mesh):
    in_specs = (
        P("links", "heads"),
        P("links", "heads"),
        P("links", "heads"),
        P("links", "heads"),
        P("links", "heads"),
        P("heads", None),
        P("heads", "links"),
    )
    out_specs = (P("links", "heads"), P("links", "heads"), P("links", "heads"))
    return jax.shard_map(body, mesh=mesh, in_specs=in_specs, out_specs=out_specs, check_vma=False)
```

```python
import jax
import jax.numpy as jnp
from jax import lax
from jax.experimental import pallas as pl
from jax.experimental.pallas import tpu as pltpu
from jax.sharding import PartitionSpec as P

F32, BF = jnp.float32, jnp.bfloat16
MESH = pl.DeviceIdType.MESH
LOG2E = 1.4426950408889634

XH, NZD, NYD = 2, 8, 4
ROWS = 1024
SHARD = 64
WIDTH = 128
DH = 64
CHUNK = 256
AUG = 256
ORDER = (4, 3, 5, 2, 6, 1, 7, 0)
PLACE = {r: i for i, r in enumerate(ORDER)}
FAR, NEAR = 0, 1
TILE = 256
HALF_R = {FAR: (4, 3, 5, 2), NEAR: (6, 1, 7)}
PIECES = 4
PROWS = ROWS // PIECES


def mm(a, b):
    return jnp.dot(a, b, preferred_element_type=F32)


def nt(a, b):
    return lax.dot_general(a, b, (((1,), (1,)), ((), ())), preferred_element_type=F32)


def three(row):
    a = row.astype(BF).astype(F32)
    b = (row - a).astype(BF).astype(F32)
    return [a, b, row - a - b]


def columns(rows):
    n = rows.shape[1]
    pad = jnp.zeros((5, n), F32)
    parts = [p for h in range(2) for p in (*three(rows[h : h + 1, :]), pad)]
    low = jnp.concatenate(parts, 0).astype(BF)
    return jnp.concatenate([low, jnp.zeros((WIDTH - 16, n), BF)], 0).T


def kernel(
    q_in, k_in, v_in, attn_in, cot_in, w_in, lse_in,
    mine_out, dqr, dk_out, dv_out,
    attn, w, in_sem, cot, qa, da, lse2, delta2, qx, dx, q_t, d_t, kv, acc, psend, precv, zsend, zrecv, owned,
    probs, grads, dq, dqs, zsend2, zrecv2, owned2, send2, recv2,
    cot_ss, cot_rs, z_ss, z_rs, y_ss, y_rs, x_ss, x_rs, r_ss, r_rs, g_ss, g_rs, dq_ss, dq_rs, t_ss, t_rs, out_sem,
):
    link, head = lax.axis_index("links"), lax.axis_index("heads")
    xh, z, y = link // (NZD * NYD), (link // NYD) % NZD, link % NYD
    xl, core = head // 2, head % 2

    def at(dxh=0, dz=0, dy=0, dxl=0, dc=0):
        return (
            ((xh + dxh) % XH) * (NZD * NYD) + ((z + dz) % NZD) * NYD + (y + dy) % NYD,
            ((xl + dxl) % 2) * 2 + (core + dc) % 2,
        )

    def copy(src, dst, ss, rs, to):
        return pltpu.make_async_remote_copy(
            src_ref=src, dst_ref=dst, send_sem=ss, recv_sem=rs, device_id=to, device_id_type=MESH
        )

    def piece(i):
        return pl.ds(i * PROWS, PROWS)

    def half_at(p):
        return pl.ds(p * 4, 4)

    partners = [at(dz=r) for r in range(1, NZD)] + [at(dy=r) for r in range(1, NYD)]
    partners += [at(dxh=1), at(dxl=1), at(dc=1)]
    barrier = pltpu.get_barrier_semaphore()
    for to in partners:
        pl.semaphore_signal(barrier, inc=1, device_id=to, device_id_type=MESH)
    places = (
        (k_in, kv.at[0, PLACE[0], 0]), (v_in, kv.at[0, PLACE[0], 1]), (q_in, qa.at[0]),
        (attn_in, attn), (lse_in, lse2.at[0]), (w_in, w), (cot_in, cot.at[0]),
    )
    fetch = [pltpu.make_async_copy(src, dst, in_sem.at[i]) for i, (src, dst) in enumerate(places)]
    for c in fetch:
        c.start()

    across = [
        copy(cot_in.at[piece(i)], cot.at[2, piece(i)], cot_ss.at[0, i], cot_rs.at[0, i], at(dxl=1))
        for i in range(PIECES)
    ]
    beside = copy(cot_in, cot.at[1], cot_ss.at[1, 0], cot_rs.at[1, 0], at(dc=1))
    onward = [
        copy(cot.at[2, piece(i)], cot.at[3, piece(i)], cot_ss.at[2, i], cot_rs.at[2, i], at(dc=1))
        for i in range(PIECES)
    ]
    shard = kv.at[0, PLACE[0]]
    along_z = {
        r: copy(shard, kv.at[0, PLACE[(NZD - r) % NZD]], z_ss.at[r], z_rs.at[r], at(dz=r))
        for r in (4, 3, 5, 2, 6, 1, 7)
    }
    def along_y(k, p):
        part = half_at(p)
        return copy(kv.at[0, part], kv.at[k, part], y_ss.at[k, p], y_rs.at[k, p], at(dy=-k))

    swap_q = copy(q_in, qa.at[1], x_ss.at[0], x_rs.at[0], at(dxh=1))
    swap_l = copy(lse_in, lse2.at[1], x_ss.at[1], x_rs.at[1], at(dxh=1))
    swap_d = copy(delta2.at[0], delta2.at[1], x_ss.at[2], x_rs.at[2], at(dxh=1))
    swap_a = [
        copy(da.at[0, piece(i)], da.at[1, piece(i)], x_ss.at[3 + i], x_rs.at[3 + i], at(dxh=1))
        for i in range(PIECES)
    ]
    def back_y(k, p):
        return copy(psend.at[k - 1, p], precv.at[k - 1, p], r_ss.at[k, p], r_rs.at[k, p], at(dy=k))

    back_z = {
        r: copy(zsend.at[PLACE[r]], zrecv.at[r - 1], g_ss.at[r], g_rs.at[r], at(dz=r))
        for r in (4, 3, 5, 2, 6, 1, 7)
    }
    back_z2 = {
        r: copy(zsend2.at[PLACE[r]], zrecv2.at[r - 1], t_ss.at[r], t_rs.at[r], at(dz=r))
        for r in (4, 3, 5, 2, 6, 1, 7)
    }
    across_y = copy(send2, recv2, t_ss.at[0], t_rs.at[0], at(dy=2))
    back_q = [
        copy(dqs.at[part], dqr.at[part], dq_ss.at[i], dq_rs.at[i], at(dxh=1))
        for i, part in enumerate((pl.ds(0, ROWS // 2), pl.ds(ROWS // 2, ROWS // 2)))
    ]

    pl.semaphore_wait(barrier, len(partners))
    for c in across:
        c.start()
    fetch[0].wait()
    fetch[1].wait()
    for p in (NEAR, FAR):
        for r in HALF_R[p]:
            along_z[NZD - r].start()
    beside.start()
    fetch[2].wait()
    fetch[4].wait()
    dq[...] = jnp.zeros_like(dq)
    acc[...] = jnp.zeros_like(acc)

    lane = lax.broadcasted_iota(jnp.int32, (1, WIDTH), 1)

    def one_head(h):
        return jnp.where(lane // DH == h, 1.0, 0.0)

    def one_group(h):
        return jnp.where(lane // 8 == h, 1.0, 0.0).astype(BF)

    def widen_q(half):
        tokens = qa[half]
        q_t[half] = (tokens * jnp.full((1, WIDTH), 0.125, BF)).T
        extra = columns(lse2[half])
        for h in range(2):
            qx[half, h, :, :WIDTH] = tokens * (one_head(h) * 0.125).astype(BF)
            qx[half, h, :, WIDTH:] = extra * one_group(h)

    def widen_d(half, rows, tokens):
        extra = columns(delta2[half, :, rows])
        for h in range(2):
            dx[half, h, rows, :WIDTH] = tokens * one_head(h).astype(BF)
            dx[half, h, rows, WIDTH:] = extra * one_group(h)

    widen_q(0)
    fetch[3].wait()
    attn_t = attn[...].T

    def pass_on(i):
        across[i].wait_recv()
        onward[i].start()

    def spread(p):
        for r in HALF_R[p]:
            along_z[NZD - r].wait_recv()
        for k in (1, 3):
            along_y(k, p).start()

    pass_on(0)
    spread(NEAR)
    pass_on(1)
    pass_on(2)
    swap_q.start()
    swap_l.start()
    pass_on(3)
    spread(FAR)
    fetch[5].wait()
    fetch[6].wait()
    beside.wait_recv()

    def block(dxl, dc):
        which = ((xl + dxl) % 2) * 2 + (core + dc) % 2
        return w[:, pl.ds(pl.multiple_of(which * WIDTH, WIDTH), WIDTH)]

    weight = jnp.concatenate([block(0, 0), block(0, 1), block(1, 0), block(1, 1)], 1)
    row = lax.broadcasted_iota(jnp.int32, (WIDTH, CHUNK), 0)
    minus = jnp.where(row < 16, -1.0, 0.0).astype(BF)
    left = lax.broadcasted_iota(jnp.int32, (TILE, WIDTH), 1) < DH
    tiles = range(ROWS // TILE)

    def unit(half, k, p):
        places = pl.ds(p * 4, 4)
        keys = kv[k, places, 0].reshape(CHUNK, WIDTH)
        values = kv[k, places, 1].reshape(CHUNK, WIDTH)
        right_k = jnp.concatenate([keys.T, minus], 0)
        right_v = jnp.concatenate([values.T, minus], 0)

        def tile(h, j):
            rows = slice(j * TILE, (j + 1) * TILE)
            scores = mm(qx[half, h, rows, :], right_k)
            moved = mm(dx[half, h, rows, :], right_v)
            prob = jnp.exp2(scores * LOG2E)
            probs[h, rows, :] = prob.astype(BF)
            grads[h, rows, :] = (prob * moved).astype(BF)

        def zones(h):
            own = slice(DH * h, DH * h + DH)
            grad_k = acc[k, p, 0, own, :] + mm(q_t[half, own, :], grads[h])
            grad_v = acc[k, p, 1, own, :] + mm(d_t[half, own, :], probs[h])
            acc[k, p, 0, own, :] = grad_k
            acc[k, p, 1, own, :] = grad_v

        def links(j):
            rows = slice(j * TILE, (j + 1) * TILE)
            dq[half, rows, :] += jnp.where(left, mm(grads[0, rows, :], keys), mm(grads[1, rows, :], keys))

        return tile, zones, links

    tile, zones, links = unit(0, 0, FAR)
    for i in range(PIECES):
        onward[i].wait_recv()
        rows = pl.ds(i * PROWS, PROWS)
        wide = jnp.concatenate([cot[0, rows], cot[1, rows], cot[2, rows], cot[3, rows]], 1)
        tokens = nt(wide, weight).astype(BF)
        da[0, rows] = tokens
        swap_a[i].start()
        turned = tokens.T
        d_t[0, :, rows] = turned
        product = turned.astype(F32) * attn_t[:, i * PROWS : (i + 1) * PROWS].astype(F32)
        for h in range(2):
            delta2[0, h : h + 1, rows] = jnp.sum(product[DH * h : DH * h + DH], axis=0, keepdims=True)
        widen_d(0, rows, tokens)
        for h in range(2):
            tile(h, i)
    swap_d.start()
    along_y(2, NEAR).start()
    along_y(2, FAR).start()
    for h in range(2):
        zones(h)
    for j in tiles:
        links(j)

    def work(half, k, p):
        tile, zones, links = unit(half, k, p)
        for j in tiles:
            tile(0, j)
        tile(1, 0)
        zones(0)
        for j in tiles[1:]:
            tile(1, j)
        zones(1)
        for j in tiles:
            links(j)

    def own_step(i, _):
        late = i // 4
        k, p = (1 + 2 * (i % 2)) * (1 - late) + 2 * late, (1 - i // 2) * (1 - late) + (5 - i) * late
        along_y(k, p).wait_recv()
        work(0, k, p)
        return 0

    lax.fori_loop(0, 6, own_step, 0)

    for c in (swap_q, swap_l, *swap_a, swap_d):
        c.wait_recv()
    widen_q(1)
    for i in range(PIECES):
        tokens = da[1, piece(i)]
        d_t[1, :, piece(i)] = tokens.T
        widen_d(1, piece(i), tokens)
    def swapped_step(i, _):
        k = jnp.where(i < 2, 2, jnp.where(i == 6, 0, 1 + 2 * (i % 2)))
        p = jnp.where(i < 2, i, jnp.where(i == 6, 0, i // 4))
        work(1, k, p)

        for part in (FAR, NEAR):

            @pl.when(i == part)
            def _():
                turn(2, part, (), zsend2, owned2)
                for r in HALF_R[part]:
                    back_z2[r].start()

        for first in (0, 1):

            @pl.when((i == 2 + first) | (i == 4 + first))
            def _():
                cls = 1 + 2 * first
                psend[cls - 1, p] = acc[cls, p].astype(BF)
                back_y(cls, p).start()

        return 0

    def turn(k, p, others, target, keep):
        for t in range(2):
            line = acc[k, p, t]
            for cls in others:
                line = line + precv[cls - 1, p, t].astype(F32)
            shards = line.T.reshape(4, SHARD, WIDTH)
            target[half_at(p), t] = shards.astype(BF)
            if p == NEAR:
                keep[t] = shards[PLACE[0] - 4]

    def gather(p):
        for cls in (1, 3):
            back_y(cls, p).wait_recv()
        turn(0, p, (1, 3), zsend, owned)
        for r in HALF_R[p]:
            back_z[r].start()

    lax.fori_loop(0, 7, swapped_step, 0)

    total = owned2[...]
    for r in HALF_R[FAR] + HALF_R[NEAR]:
        back_z2[r].wait_recv()
        total = total + zrecv2[r - 1].astype(F32)
    send2[...] = total.astype(BF)
    across_y.start()
    gather(FAR)

    tile, zones, links = unit(1, 0, NEAR)
    for i in range(2):
        for j in tiles[2 * i : 2 * i + 2]:
            for h in range(2):
                tile(h, j)
        for j in tiles[2 * i : 2 * i + 2]:
            links(j)
        rows = slice(i * (ROWS // 2), (i + 1) * (ROWS // 2))
        dqs[rows, :] = (dq[1, rows, :] * 0.125).astype(BF)
        back_q[i].start()
    for h in range(2):
        zones(h)

    work(0, 0, NEAR)

    out = pltpu.make_async_copy(dq.at[0], mine_out, out_sem)
    out.start()
    gather(NEAR)
    total = owned[...]
    across_y.wait_recv()
    total = total + recv2[...].astype(F32)
    for r in HALF_R[FAR] + HALF_R[NEAR]:
        back_z[r].wait_recv()
        total = total + zrecv[r - 1].astype(F32)
    dk_out[...] = total[0].astype(BF)
    dv_out[...] = total[1].astype(BF)
    for c in back_q:
        c.wait_recv()
    out.wait()

    for c in (
        *across, beside, *onward, *along_z.values(), swap_q, swap_l, swap_d, *swap_a,
        *back_z.values(), *back_z2.values(), across_y, *back_q,
        *(along_y(k, p) for k in (1, 2, 3) for p in (FAR, NEAR)),
        *(back_y(k, p) for k in (1, 3) for p in (FAR, NEAR)),
    ):
        c.wait_send()


def body(queries, keys, values, attn, cotangent, out_weight, lse):
    vmem = pl.BlockSpec(memory_space=pltpu.VMEM)
    dma = pltpu.SemaphoreType.DMA
    anywhere = pl.BlockSpec(memory_space=pl.ANY)
    mine, returned, key_grad, value_grad = pl.pallas_call(
        kernel,
        out_shape=[
            jax.ShapeDtypeStruct((ROWS, WIDTH), F32),
            jax.ShapeDtypeStruct((ROWS, WIDTH), BF),
            jax.ShapeDtypeStruct((SHARD, WIDTH), BF),
            jax.ShapeDtypeStruct((SHARD, WIDTH), BF),
        ],
        in_specs=[anywhere] * 7,
        out_specs=[anywhere, anywhere, vmem, vmem],
        scratch_shapes=[
            pltpu.VMEM((ROWS, WIDTH), BF),
            pltpu.VMEM((WIDTH, 4 * WIDTH), BF),
            dma((7,)),
            pltpu.VMEM((4, ROWS, WIDTH), BF),
            pltpu.VMEM((2, ROWS, WIDTH), BF),
            pltpu.VMEM((2, ROWS, WIDTH), BF),
            pltpu.VMEM((2, 2, ROWS), F32),
            pltpu.VMEM((2, 2, ROWS), F32),
            pltpu.VMEM((2, 2, ROWS, AUG), BF),
            pltpu.VMEM((2, 2, ROWS, AUG), BF),
            pltpu.VMEM((2, WIDTH, ROWS), BF),
            pltpu.VMEM((2, WIDTH, ROWS), BF),
            pltpu.VMEM((4, NZD, 2, SHARD, WIDTH), BF),
            pltpu.VMEM((4, 2, 2, WIDTH, CHUNK), F32),
            pltpu.VMEM((3, 2, 2, WIDTH, CHUNK), BF),
            pltpu.VMEM((3, 2, 2, WIDTH, CHUNK), BF),
            pltpu.VMEM((NZD, 2, SHARD, WIDTH), BF),
            pltpu.VMEM((NZD - 1, 2, SHARD, WIDTH), BF),
            pltpu.VMEM((2, SHARD, WIDTH), F32),
            pltpu.VMEM((2, ROWS, CHUNK), BF),
            pltpu.VMEM((2, ROWS, CHUNK), BF),
            pltpu.VMEM((2, ROWS, WIDTH), F32),
            pltpu.VMEM((ROWS, WIDTH), BF),
            pltpu.VMEM((NZD, 2, SHARD, WIDTH), BF),
            pltpu.VMEM((NZD - 1, 2, SHARD, WIDTH), BF),
            pltpu.VMEM((2, SHARD, WIDTH), F32),
            pltpu.VMEM((2, SHARD, WIDTH), BF),
            pltpu.VMEM((2, SHARD, WIDTH), BF),
            dma((3, PIECES)), dma((3, PIECES)),
            dma((NZD,)), dma((NZD,)),
            dma((4, 2)), dma((4, 2)),
            dma((3 + PIECES,)), dma((3 + PIECES,)),
            dma((4, 2)), dma((4, 2)),
            dma((NZD,)), dma((NZD,)),
            dma((2,)), dma((2,)),
            dma((NZD,)), dma((NZD,)),
            dma,
        ],
        compiler_params=pltpu.CompilerParams(
            collective_id=0, has_side_effects=True, vmem_limit_bytes=56 * 2**20
        ),
        cost_estimate=pl.CostEstimate(
            flops=11 * 10**9, bytes_accessed=3 * 2**20, transcendentals=2**23
        ),
    )(queries, keys, values, attn, cotangent, out_weight, lse)
    return (mine * 0.125 + returned.astype(F32)).astype(BF), key_grad, value_grad


def solution(mesh):
    in_specs = (
        P("links", "heads"),
        P("links", "heads"),
        P("links", "heads"),
        P("links", "heads"),
        P("links", "heads"),
        P("heads", None),
        P("heads", "links"),
    )
    out_specs = (P("links", "heads"), P("links", "heads"), P("links", "heads"))
    return jax.shard_map(body, mesh=mesh, in_specs=in_specs, out_specs=out_specs, check_vma=False)
```

```python
import jax
import jax.numpy as jnp
from jax import lax
from jax.experimental import pallas as pl
from jax.experimental.pallas import tpu as pltpu
from jax.sharding import PartitionSpec as P

F32, BF = jnp.float32, jnp.bfloat16
MESH = pl.DeviceIdType.MESH
LOG2E = 1.4426950408889634

XH, NZD, NYD = 2, 8, 4
ROWS = 1024
SHARD = 64
WIDTH = 128
DH = 64
CHUNK = 256
AUG = 256
ORDER = (4, 3, 5, 2, 6, 1, 7, 0)
PLACE = {r: i for i, r in enumerate(ORDER)}
FAR, NEAR = 0, 1
TILE = 256
HALF_R = {FAR: (4, 3, 5, 2), NEAR: (6, 1, 7)}
PIECES = 4
PROWS = ROWS // PIECES


def mm(a, b):
    return jnp.dot(a, b, preferred_element_type=F32)


def nt(a, b):
    return lax.dot_general(a, b, (((1,), (1,)), ((), ())), preferred_element_type=F32)


def three(row):
    a = row.astype(BF).astype(F32)
    b = (row - a).astype(BF).astype(F32)
    return [a, b, row - a - b]


def columns(rows):
    n = rows.shape[1]
    pad = jnp.zeros((5, n), F32)
    parts = [p for h in range(2) for p in (*three(rows[h : h + 1, :]), pad)]
    low = jnp.concatenate(parts, 0).astype(BF)
    return jnp.concatenate([low, jnp.zeros((WIDTH - 16, n), BF)], 0).T


def kernel(
    q_in, k_in, v_in, attn_in, cot_in, w_in, lse_in,
    mine_out, dqr, dk_out, dv_out,
    attn, w, in_sem, cot, qa, da, lse2, delta2, qx, dx, q_t, d_t, kv, acc, psend, precv, zsend, zrecv, owned,
    probs, grads, dq, dqs, zsend2, zrecv2, owned2, send2, recv2,
    cot_ss, cot_rs, z_ss, z_rs, y_ss, y_rs, x_ss, x_rs, r_ss, r_rs, g_ss, g_rs, dq_ss, dq_rs, t_ss, t_rs, out_sem,
):
    link, head = lax.axis_index("links"), lax.axis_index("heads")
    xh, z, y = link // (NZD * NYD), (link // NYD) % NZD, link % NYD
    xl, core = head // 2, head % 2

    def at(dxh=0, dz=0, dy=0, dxl=0, dc=0):
        return (
            ((xh + dxh) % XH) * (NZD * NYD) + ((z + dz) % NZD) * NYD + (y + dy) % NYD,
            ((xl + dxl) % 2) * 2 + (core + dc) % 2,
        )

    def copy(src, dst, ss, rs, to):
        return pltpu.make_async_remote_copy(
            src_ref=src, dst_ref=dst, send_sem=ss, recv_sem=rs, device_id=to, device_id_type=MESH
        )

    def piece(i):
        return pl.ds(i * PROWS, PROWS)

    def half_at(p):
        return pl.ds(p * 4, 4)

    partners = [at(dz=r) for r in range(1, NZD)] + [at(dy=r) for r in range(1, NYD)]
    partners += [at(dxh=1), at(dxl=1), at(dc=1)]
    barrier = pltpu.get_barrier_semaphore()
    for to in partners:
        pl.semaphore_signal(barrier, inc=1, device_id=to, device_id_type=MESH)
    places = (
        (k_in, kv.at[0, PLACE[0], 0]), (v_in, kv.at[0, PLACE[0], 1]), (q_in, qa.at[0]),
        (attn_in, attn), (lse_in, lse2.at[0]), (w_in, w), (cot_in, cot.at[0]),
    )
    fetch = [pltpu.make_async_copy(src, dst, in_sem.at[i]) for i, (src, dst) in enumerate(places)]
    for c in fetch:
        c.start()

    across = [
        copy(cot_in.at[piece(i)], cot.at[2, piece(i)], cot_ss.at[0, i], cot_rs.at[0, i], at(dxl=1))
        for i in range(PIECES)
    ]
    beside = copy(cot_in, cot.at[1], cot_ss.at[1, 0], cot_rs.at[1, 0], at(dc=1))
    onward = [
        copy(cot.at[2, piece(i)], cot.at[3, piece(i)], cot_ss.at[2, i], cot_rs.at[2, i], at(dc=1))
        for i in range(PIECES)
    ]
    shard = kv.at[0, PLACE[0]]
    along_z = {
        r: copy(shard, kv.at[0, PLACE[(NZD - r) % NZD]], z_ss.at[r], z_rs.at[r], at(dz=r))
        for r in (4, 3, 5, 2, 6, 1, 7)
    }
    def along_y(k, p):
        part = half_at(p)
        return copy(kv.at[0, part], kv.at[k, part], y_ss.at[k, p], y_rs.at[k, p], at(dy=-k))

    swap_q = copy(q_in, qa.at[1], x_ss.at[0], x_rs.at[0], at(dxh=1))
    swap_l = copy(lse_in, lse2.at[1], x_ss.at[1], x_rs.at[1], at(dxh=1))
    swap_d = copy(delta2.at[0], delta2.at[1], x_ss.at[2], x_rs.at[2], at(dxh=1))
    swap_a = [
        copy(da.at[0, piece(i)], da.at[1, piece(i)], x_ss.at[3 + i], x_rs.at[3 + i], at(dxh=1))
        for i in range(PIECES)
    ]
    def back_y(k, p):
        return copy(psend.at[k - 1, p], precv.at[k - 1, p], r_ss.at[k, p], r_rs.at[k, p], at(dy=k))

    back_z = {
        r: copy(zsend.at[PLACE[r]], zrecv.at[r - 1], g_ss.at[r], g_rs.at[r], at(dz=r))
        for r in (4, 3, 5, 2, 6, 1, 7)
    }
    back_z2 = {
        r: copy(zsend2.at[PLACE[r]], zrecv2.at[r - 1], t_ss.at[r], t_rs.at[r], at(dz=r))
        for r in (4, 3, 5, 2, 6, 1, 7)
    }
    across_y = copy(send2, recv2, t_ss.at[0], t_rs.at[0], at(dy=2))
    back_q = [
        copy(dqs.at[part], dqr.at[part], dq_ss.at[i], dq_rs.at[i], at(dxh=1))
        for i, part in enumerate((pl.ds(0, ROWS // 2), pl.ds(ROWS // 2, ROWS // 2)))
    ]

    pl.semaphore_wait(barrier, len(partners))
    for c in across:
        c.start()
    fetch[0].wait()
    fetch[1].wait()
    for p in (NEAR, FAR):
        for r in HALF_R[p]:
            along_z[NZD - r].start()
    beside.start()
    fetch[2].wait()
    fetch[4].wait()
    dq[...] = jnp.zeros_like(dq)
    acc[...] = jnp.zeros_like(acc)

    lane = lax.broadcasted_iota(jnp.int32, (1, WIDTH), 1)

    def one_head(h):
        return jnp.where(lane // DH == h, 1.0, 0.0)

    def one_group(h):
        return jnp.where(lane // 8 == h, 1.0, 0.0).astype(BF)

    def widen_q(half):
        tokens = qa[half]
        q_t[half] = (tokens * jnp.full((1, WIDTH), 0.125, BF)).T
        extra = columns(lse2[half])
        for h in range(2):
            qx[half, h, :, :WIDTH] = tokens * (one_head(h) * 0.125).astype(BF)
            qx[half, h, :, WIDTH:] = extra * one_group(h)

    def widen_d(half, rows, tokens):
        extra = columns(delta2[half, :, rows])
        for h in range(2):
            dx[half, h, rows, :WIDTH] = tokens * one_head(h).astype(BF)
            dx[half, h, rows, WIDTH:] = extra * one_group(h)

    widen_q(0)
    fetch[3].wait()
    attn_t = attn[...].T

    def pass_on(i):
        across[i].wait_recv()
        onward[i].start()

    def spread(p):
        for r in HALF_R[p]:
            along_z[NZD - r].wait_recv()
        for k in (1, 3):
            along_y(k, p).start()

    pass_on(0)
    spread(NEAR)
    pass_on(1)
    pass_on(2)
    swap_q.start()
    swap_l.start()
    pass_on(3)
    spread(FAR)
    fetch[5].wait()
    fetch[6].wait()
    beside.wait_recv()

    def block(dxl, dc):
        which = ((xl + dxl) % 2) * 2 + (core + dc) % 2
        return w[:, pl.ds(pl.multiple_of(which * WIDTH, WIDTH), WIDTH)]

    weight = jnp.concatenate([block(0, 0), block(0, 1), block(1, 0), block(1, 1)], 1)
    row = lax.broadcasted_iota(jnp.int32, (WIDTH, CHUNK), 0)
    minus = jnp.where(row < 16, -1.0, 0.0).astype(BF)
    left = lax.broadcasted_iota(jnp.int32, (TILE, WIDTH), 1) < DH
    tiles = range(ROWS // TILE)

    def unit(half, k, p):
        places = pl.ds(p * 4, 4)
        keys = kv[k, places, 0].reshape(CHUNK, WIDTH)
        values = kv[k, places, 1].reshape(CHUNK, WIDTH)
        right_k = jnp.concatenate([keys.T, minus], 0)
        right_v = jnp.concatenate([values.T, minus], 0)

        def tile(h, j):
            rows = slice(j * TILE, (j + 1) * TILE)
            scores = mm(qx[half, h, rows, :], right_k)
            moved = mm(dx[half, h, rows, :], right_v)
            prob = jnp.exp2(scores * LOG2E)
            probs[h, rows, :] = prob.astype(BF)
            grads[h, rows, :] = (prob * moved).astype(BF)

        def zones(h):
            own = slice(DH * h, DH * h + DH)
            grad_k = acc[k, p, 0, own, :] + mm(q_t[half, own, :], grads[h])
            grad_v = acc[k, p, 1, own, :] + mm(d_t[half, own, :], probs[h])
            acc[k, p, 0, own, :] = grad_k
            acc[k, p, 1, own, :] = grad_v

        def links(j):
            rows = slice(j * TILE, (j + 1) * TILE)
            dq[half, rows, :] += jnp.where(left, mm(grads[0, rows, :], keys), mm(grads[1, rows, :], keys))

        return tile, zones, links

    tile, zones, links = unit(0, 0, FAR)
    for i in range(PIECES):
        onward[i].wait_recv()
        rows = pl.ds(i * PROWS, PROWS)
        wide = jnp.concatenate([cot[0, rows], cot[1, rows], cot[2, rows], cot[3, rows]], 1)
        tokens = nt(wide, weight).astype(BF)
        da[0, rows] = tokens
        swap_a[i].start()
        turned = tokens.T
        d_t[0, :, rows] = turned
        product = turned.astype(F32) * attn_t[:, i * PROWS : (i + 1) * PROWS].astype(F32)
        for h in range(2):
            delta2[0, h : h + 1, rows] = jnp.sum(product[DH * h : DH * h + DH], axis=0, keepdims=True)
        widen_d(0, rows, tokens)
        for h in range(2):
            tile(h, i)
    swap_d.start()
    along_y(2, NEAR).start()
    along_y(2, FAR).start()
    for h in range(2):
        zones(h)
    for j in tiles:
        links(j)

    def work(half, k, p):
        tile, zones, links = unit(half, k, p)
        for j in tiles:
            tile(0, j)
        tile(1, 0)
        zones(0)
        for j in tiles[1:]:
            tile(1, j)
        zones(1)
        for j in tiles:
            links(j)

    def own_step(i, _):
        late = i // 4
        k, p = (1 + 2 * (i % 2)) * (1 - late) + 2 * late, (1 - i // 2) * (1 - late) + (5 - i) * late
        along_y(k, p).wait_recv()
        work(0, k, p)
        return 0

    lax.fori_loop(0, 6, own_step, 0)

    for c in (swap_q, swap_l, *swap_a, swap_d):
        c.wait_recv()
    widen_q(1)
    for i in range(PIECES):
        tokens = da[1, piece(i)]
        d_t[1, :, piece(i)] = tokens.T
        widen_d(1, piece(i), tokens)
    def swapped_step(i, _):
        k = jnp.where(i < 2, 2, jnp.where(i == 6, 0, 1 + 2 * (i % 2)))
        p = jnp.where(i < 2, i, jnp.where(i == 6, 0, i // 4))
        work(1, k, p)

        for part in (FAR, NEAR):

            @pl.when(i == part)
            def _():
                turn(2, part, (), zsend2, owned2)
                for r in HALF_R[part]:
                    back_z2[r].start()

        for first in (0, 1):

            @pl.when((i == 2 + first) | (i == 4 + first))
            def _():
                cls = 1 + 2 * first
                psend[cls - 1, p] = acc[cls, p].astype(BF)
                back_y(cls, p).start()

        return 0

    def turn(k, p, others, target, keep):
        for t in range(2):
            line = acc[k, p, t]
            for cls in others:
                line = line + precv[cls - 1, p, t].astype(F32)
            shards = line.T.reshape(4, SHARD, WIDTH)
            target[half_at(p), t] = shards.astype(BF)
            if p == NEAR:
                keep[t] = shards[PLACE[0] - 4]

    def gather(p):
        for cls in (1, 3):
            back_y(cls, p).wait_recv()
        turn(0, p, (1, 3), zsend, owned)
        for r in HALF_R[p]:
            back_z[r].start()

    lax.fori_loop(0, 7, swapped_step, 0)

    total = owned2[...]
    for r in HALF_R[FAR] + HALF_R[NEAR]:
        back_z2[r].wait_recv()
        total = total + zrecv2[r - 1].astype(F32)
    send2[...] = total.astype(BF)
    across_y.start()
    gather(FAR)

    tile, zones, links = unit(1, 0, NEAR)
    for i in range(2):
        for j in tiles[2 * i : 2 * i + 2]:
            for h in range(2):
                tile(h, j)
        for j in tiles[2 * i : 2 * i + 2]:
            links(j)
        rows = slice(i * (ROWS // 2), (i + 1) * (ROWS // 2))
        dqs[rows, :] = (dq[1, rows, :] * 0.125).astype(BF)
        back_q[i].start()
    for h in range(2):
        zones(h)

    work(0, 0, NEAR)

    out = pltpu.make_async_copy(dq.at[0], mine_out, out_sem)
    out.start()
    gather(NEAR)
    for c in (
        *across, beside, *onward, *along_z.values(), swap_q, swap_l, swap_d, *swap_a,
        *back_z2.values(), across_y,
        *(along_y(k, p) for k in (1, 2, 3) for p in (FAR, NEAR)),
        *(back_y(k, p) for k in (1, 3) for p in (FAR, NEAR)),
    ):
        c.wait_send()
    total = owned[...]
    across_y.wait_recv()
    total = total + recv2[...].astype(F32)
    for r in HALF_R[FAR] + HALF_R[NEAR]:
        back_z[r].wait_recv()
        total = total + zrecv[r - 1].astype(F32)
    dk_out[...] = total[0].astype(BF)
    dv_out[...] = total[1].astype(BF)
    for c in back_q:
        c.wait_recv()
    out.wait()

    for c in (*back_z.values(), *back_q):
        c.wait_send()


def body(queries, keys, values, attn, cotangent, out_weight, lse):
    vmem = pl.BlockSpec(memory_space=pltpu.VMEM)
    dma = pltpu.SemaphoreType.DMA
    anywhere = pl.BlockSpec(memory_space=pl.ANY)
    mine, returned, key_grad, value_grad = pl.pallas_call(
        kernel,
        out_shape=[
            jax.ShapeDtypeStruct((ROWS, WIDTH), F32),
            jax.ShapeDtypeStruct((ROWS, WIDTH), BF),
            jax.ShapeDtypeStruct((SHARD, WIDTH), BF),
            jax.ShapeDtypeStruct((SHARD, WIDTH), BF),
        ],
        in_specs=[anywhere] * 7,
        out_specs=[anywhere, anywhere, vmem, vmem],
        scratch_shapes=[
            pltpu.VMEM((ROWS, WIDTH), BF),
            pltpu.VMEM((WIDTH, 4 * WIDTH), BF),
            dma((7,)),
            pltpu.VMEM((4, ROWS, WIDTH), BF),
            pltpu.VMEM((2, ROWS, WIDTH), BF),
            pltpu.VMEM((2, ROWS, WIDTH), BF),
            pltpu.VMEM((2, 2, ROWS), F32),
            pltpu.VMEM((2, 2, ROWS), F32),
            pltpu.VMEM((2, 2, ROWS, AUG), BF),
            pltpu.VMEM((2, 2, ROWS, AUG), BF),
            pltpu.VMEM((2, WIDTH, ROWS), BF),
            pltpu.VMEM((2, WIDTH, ROWS), BF),
            pltpu.VMEM((4, NZD, 2, SHARD, WIDTH), BF),
            pltpu.VMEM((4, 2, 2, WIDTH, CHUNK), F32),
            pltpu.VMEM((3, 2, 2, WIDTH, CHUNK), BF),
            pltpu.VMEM((3, 2, 2, WIDTH, CHUNK), BF),
            pltpu.VMEM((NZD, 2, SHARD, WIDTH), BF),
            pltpu.VMEM((NZD - 1, 2, SHARD, WIDTH), BF),
            pltpu.VMEM((2, SHARD, WIDTH), F32),
            pltpu.VMEM((2, ROWS, CHUNK), BF),
            pltpu.VMEM((2, ROWS, CHUNK), BF),
            pltpu.VMEM((2, ROWS, WIDTH), F32),
            pltpu.VMEM((ROWS, WIDTH), BF),
            pltpu.VMEM((NZD, 2, SHARD, WIDTH), BF),
            pltpu.VMEM((NZD - 1, 2, SHARD, WIDTH), BF),
            pltpu.VMEM((2, SHARD, WIDTH), F32),
            pltpu.VMEM((2, SHARD, WIDTH), BF),
            pltpu.VMEM((2, SHARD, WIDTH), BF),
            dma((3, PIECES)), dma((3, PIECES)),
            dma((NZD,)), dma((NZD,)),
            dma((4, 2)), dma((4, 2)),
            dma((3 + PIECES,)), dma((3 + PIECES,)),
            dma((4, 2)), dma((4, 2)),
            dma((NZD,)), dma((NZD,)),
            dma((2,)), dma((2,)),
            dma((NZD,)), dma((NZD,)),
            dma,
        ],
        compiler_params=pltpu.CompilerParams(
            collective_id=0, has_side_effects=True, vmem_limit_bytes=56 * 2**20
        ),
        cost_estimate=pl.CostEstimate(
            flops=11 * 10**9, bytes_accessed=3 * 2**20, transcendentals=2**23
        ),
    )(queries, keys, values, attn, cotangent, out_weight, lse)
    return (mine * 0.125 + returned.astype(F32)).astype(BF), key_grad, value_grad


def solution(mesh):
    in_specs = (
        P("links", "heads"),
        P("links", "heads"),
        P("links", "heads"),
        P("links", "heads"),
        P("links", "heads"),
        P("heads", None),
        P("heads", "links"),
    )
    out_specs = (P("links", "heads"), P("links", "heads"), P("links", "heads"))
    return jax.shard_map(body, mesh=mesh, in_specs=in_specs, out_specs=out_specs, check_vma=False)
```
